32 devices in a mesh: groups: 2 (over y), adapter: 8 (over z, x), tensor: 2 (over core).
Axes of the slice: x: 2, y: 2, z: 4, core: 2. Of those that a mesh axis runs over, the one named last changes fastest.
Arguments:
- hidden: bfloat16 [2048, 8192], P(('groups', 'adapter'), 'tensor'), parts along dimension 0, may hold values from -6 to 6
- row_adapter_index: int32 [2048, 1], P(('groups', 'adapter')), parts along dimension 0, may hold values from 0 to 7; in each aligned block of 128 rows (0 to 127, 128 to 255, ...) at most 32 rows name the same one
- adapter_shrink_weight: bfloat16 [8, 8192, 128], P('adapter', 'tensor'), may hold values from -0.0625 to 0.0625
- adapter_expand_weight: bfloat16 [8, 2, 64, 1024], P('adapter', None, None, 'tensor'), may hold values from -0.75 to 0.75
- base_partial_sums: bfloat16 [2, 2048, 2, 1024], P('tensor', ('groups', 'adapter')), parts along dimension 1, may hold values from -4 to 4
Outputs:
- kv_out: bfloat16 [2048, 2, 1024], P(('groups', 'adapter'), None, 'tensor'), parts along dimension 0
The draws below stay inside these ranges and needn't reach their ends.
There are 2 independent parts, one for each index of `groups`. The reference program is written for one: setup_inputs(seed, part) draws one part's arguments, and reference() takes and returns one part's arrays. A program takes and returns all parts, laid end to end along the dimension named above; an argument that names none is the same for every part. Nothing has to cross between parts.
Inputs may be any that keep to these rules, and one draw needn't show every extreme that they name: `row_adapter_index`: within each aligned block of 128 rows (the rows of one device) no adapter is named by more than 32 rows, and this bound is reached.
All inputs are finite; a program needn't handle non-finite values.
Results may differ from the reference program's by a relative error of at most 0.006.
Values may be sent and summed in bfloat16 or wider, within the bound.
A program may use at most 64 MiB of HBM per device.

```python
import math
import jax
import jax.numpy as jnp
import numpy as np
from jax import lax

MODEL_WIDTH = 8192
KEY_VALUE_WIDTH = 1024
ADAPTER_RANK = 64
ROWS_DEV = 128
ADAPTER_SLOTS = 8
ROWS = 1024
CAP = 32
N_TENSOR = 2


def shard_levels(own_key, shape, cuts, low, largest):
    def one(dim, parts):
        steps = jax.random.uniform(jax.random.fold_in(jax.random.fold_in(own_key, 6), dim), (parts,), jnp.float32, low / len(cuts), largest / len(cuts))
        return jnp.repeat(jnp.exp(steps), shape[dim] // parts).reshape((-1,) + (1,) * (len(shape) - dim - 1))

    level = one(*cuts[0])
    for cut in cuts[1:]:
        level = level * one(*cut)
    return level


def shared_out(key, own, number, rows, amount, top, bound, slope):
    order = jax.random.permutation(key, amount)
    crowded, usual = portions_of(amount, rows * top, bound, slope, True), portions_of(amount, rows * top, bound, slope, False)
    places = jnp.arange(amount)

    def named(sizes, rotation):
        used = int((sizes > 0).sum())
        fixed = max(1, used // 4)
        moved = fixed + (places - fixed + rotation * (used - fixed)) % max(1, amount - fixed)
        return jnp.zeros((amount,), jnp.int32).at[order[jnp.where(places < fixed, places, moved)]].set(jnp.asarray(sizes, jnp.int32))

    sizes = jnp.where(number % 4 == 0, named(crowded, number // 4), named(usual, number - number // 4 - 1))
    mixed = jax.random.permutation(jax.random.fold_in(own, 3), amount)
    donor, receiver = mixed[0:amount // 2 * 2:2], mixed[1:amount // 2 * 2:2]
    room = jnp.minimum(sizes[donor] - 1, bound - sizes[receiver]) // 2
    room = jnp.where((donor == order[0]) | (receiver == order[0]) | (sizes[receiver] == 0), 0, jnp.maximum(room, 0))
    moved = jax.random.randint(jax.random.fold_in(own, 4), (amount // 2,), 0, 1 << 20) % (room + 1)
    sizes = sizes.at[donor].add(-moved).at[receiver].add(moved)
    members = jnp.searchsorted(jnp.cumsum(sizes), jnp.arange(rows * top), side="right").astype(jnp.int32)
    listing = members.reshape(top, rows).T
    listing = listing[jax.random.permutation(jax.random.fold_in(own, 1), rows)]
    rotation = jax.random.randint(jax.random.fold_in(own, 2), (rows, 1), 0, top)
    return jnp.take_along_axis(listing, (jnp.arange(top)[None, :] + rotation) % top, axis=1)


def portions_of(number_of, total, bound, slope, full):
    portions = [(1 << 20) // math.isqrt(grade ** slope) + 1 for grade in range(1, number_of + 1)]
    largest = bound if full else min(bound, max(-(-total // number_of), total * portions[0] // sum(portions)))
    least = 1 if total - largest >= number_of - 1 else 0
    given, rest = [largest] + [least] * (number_of - 1), total - largest - least * (number_of - 1)
    while rest > 0:
        free = [i for i in range(1, number_of) if given[i] < largest] or [i for i in range(1, number_of) if given[i] < bound]
        whole, remaining = sum([portions[i] for i in free]), rest
        for i in free:
            extra = min(bound - given[i], max(1, remaining * portions[i] // whole), rest)
            given[i] = given[i] + extra
            rest = rest - extra
    return np.array(given)


def gaussian(key, dims, width, bound, pieces=(), dtype=jnp.bfloat16):
    values = jax.random.normal(key, dims, jnp.float32) * width
    if len(pieces) > 0:
        values = shard_levels(key, dims, pieces, -0.22, 0.18) * values
    return jnp.clip(values, min=-bound, max=bound).astype(dtype)


def setup_inputs(seed: int = 0, part: int = 0) -> dict:
    arg_keys = jax.random.split(jax.random.key(seed), 6)
    own_keys = jax.random.split(jax.random.fold_in(arg_keys[5], part), 6)
    hidden = gaussian(own_keys[0], (ROWS, MODEL_WIDTH), 1.0, 6.0, ((0, 8), (1, 2)))
    row_adapter_index_keys = jax.random.split(jax.random.fold_in(own_keys[1], 1), ROWS // ROWS_DEV)
    row_adapter_index_turns = jax.random.permutation(jax.random.fold_in(own_keys[1], 3), ROWS // ROWS_DEV)
    row_adapter_index = jax.vmap(lambda own, number: shared_out(jax.random.fold_in(own_keys[1], 2), own, number, ROWS_DEV, ADAPTER_SLOTS, 1, CAP, 2))(row_adapter_index_keys, row_adapter_index_turns).reshape((ROWS, 1))
    adapter_shrink_weight = gaussian(arg_keys[2], (ADAPTER_SLOTS, MODEL_WIDTH, 2 * ADAPTER_RANK), MODEL_WIDTH ** -0.5, 0.0625, ((0, 8), (1, 2)))
    adapter_expand_weight = gaussian(arg_keys[3], (ADAPTER_SLOTS, 2, ADAPTER_RANK, KEY_VALUE_WIDTH), ADAPTER_RANK ** -0.5, 0.75, ((0, 8), (3, 2)))
    base_partial_sums = gaussian(own_keys[4], (N_TENSOR, ROWS, 2, KEY_VALUE_WIDTH), 0.5, 4.0, ((0, 2), (1, 8)))
    return {"hidden": hidden, "row_adapter_index": row_adapter_index, "adapter_shrink_weight": adapter_shrink_weight, "adapter_expand_weight": adapter_expand_weight, "base_partial_sums": base_partial_sums}


def reference(hidden, row_adapter_index, adapter_shrink_weight, adapter_expand_weight, base_partial_sums):
    base = jnp.sum(base_partial_sums.astype(jnp.float32), axis=0)
    row_owner = row_adapter_index[:, 0]
    block_rows = 16
    block_count = ROWS // block_rows

    def one_block(operands):
        rows_block, owning_block = operands
        shrink_row_block = adapter_shrink_weight[owning_block].astype(jnp.float32)
        shrunk = jnp.einsum("rd,rdk->rk", rows_block.astype(jnp.float32), shrink_row_block, precision=lax.Precision.HIGHEST)
        expand_row_block = adapter_expand_weight[owning_block].astype(jnp.float32)
        shrunk = shrunk.reshape(block_rows, 2, ADAPTER_RANK)
        return jnp.einsum("rjk,rjkf->rjf", shrunk, expand_row_block, precision=lax.Precision.HIGHEST)

    delta = lax.map(one_block, (hidden.reshape(block_count, block_rows, MODEL_WIDTH), row_owner.reshape(block_count, block_rows)))
    delta = delta.reshape(ROWS, 2, KEY_VALUE_WIDTH)
    return (base + delta).astype(jnp.bfloat16)
```

```python
import functools

import jax
import jax.numpy as jnp
from jax import lax
from jax.experimental import pallas as pl
from jax.experimental.pallas import tpu as pltpu
from jax.sharding import PartitionSpec as P

MESH = pl.DeviceIdType.MESH


def plane_kernel(
    nz, hidden_ref, idx_ref, w_ref, e_ref, base_ref, delta_ref, peer_base_ref,
    hbuf, mbuf, wbuf, ebuf, acc, pbuf, rbuf,
    hs, hr, ms, mr, wxs, wxr, wzs, wzr, ezs, ezr, eps, epr, ps, pr, bs, br, ls,
):
    y = lax.axis_index("groups")
    a = lax.axis_index("adapter")
    t = lax.axis_index("tensor")
    z = a // 2
    x = a % 2
    rows = hidden_ref.shape[0]
    chunk = hidden_ref.shape[1] // 4
    rank = e_ref.shape[2]
    feats = e_ref.shape[3]
    width = w_ref.shape[2]

    def coords(d):
        return (1 - x if d // 2 else x), (1 - y if d % 2 else y)

    def device(d, other=0):
        xx, yy = coords(d)
        return {"groups": yy, "adapter": 2 * z + xx, "tensor": 1 - t if other else t}

    def along(step):
        return {"groups": y, "adapter": 2 * (z + step) + x, "tensor": t}

    def quarter(d):
        xx, yy = coords(d)
        return pl.ds(pl.multiple_of((2 * xx + yy) * chunk, chunk), chunk)

    def remote(src, dst, send, recv, dev):
        return pltpu.make_async_remote_copy(
            src_ref=src, dst_ref=dst, send_sem=send, recv_sem=recv, device_id=dev, device_id_type=MESH
        )

    has_up = z < nz - 1
    has_down = z > 0
    barrier = pltpu.get_barrier_semaphore()
    for d in range(4):
        for other in range(2):
            if d or other:
                pl.semaphore_signal(barrier, inc=1, device_id=device(d, other), device_id_type=MESH)

    @pl.when(has_up)
    def _():
        pl.semaphore_signal(barrier, inc=1, device_id=along(1), device_id_type=MESH)

    @pl.when(has_down)
    def _():
        pl.semaphore_signal(barrier, inc=1, device_id=along(-1), device_id_type=MESH)

    local_h = pltpu.make_async_copy(hidden_ref.at[:, quarter(0)], hbuf.at[0], ls.at[0])
    local_w = pltpu.make_async_copy(w_ref.at[0, quarter(0)], wbuf.at[z, 0], ls.at[1])
    slot = pl.ds(pl.multiple_of(a * rank, rank), rank)
    local_e = [pltpu.make_async_copy(e_ref.at[0, j], ebuf.at[j, slot], ls.at[2 + j]) for j in range(2)]
    local_h.start()
    local_w.start()
    for copy in local_e:
        copy.start()
    mbuf[0] = jnp.broadcast_to(idx_ref[...].astype(jnp.float32), (width, rows)).T.astype(jnp.bfloat16)
    acc[...] = jnp.zeros_like(acc)
    pl.semaphore_wait(barrier, 7 + has_up.astype(jnp.int32) + has_down.astype(jnp.int32))

    def w_cross():
        return remote(w_ref.at[0, quarter(2)], wbuf.at[z, 1], wxs, wxr, device(2))

    def w_chain(way, zp, xr, own=False):
        src = w_ref.at[0, quarter(0)] if own and xr == 0 else wbuf.at[zp, xr]
        return remote(src, wbuf.at[zp, xr], wzs.at[way, zp, xr], wzr.at[zp, xr], along(1 - 2 * way))

    def e_slot(zp):
        return ebuf.at[y, pl.ds(pl.multiple_of((2 * zp + x) * rank, rank), rank)]

    def e_chain(way, zp, own=False):
        src = e_ref.at[0, y] if own else e_slot(zp)
        return remote(src, e_slot(zp), ezs.at[way, zp], ezr.at[zp], along(1 - 2 * way))

    def e_plane(d, zp, own=False):
        src = e_ref.at[0, y] if own else e_slot(zp)
        return remote(src, e_slot(zp), eps.at[zp, d], epr.at[zp, d], device(d))

    def h_copy(d):
        return remote(hidden_ref.at[:, quarter(d)], hbuf.at[d], hs.at[d], hr.at[d], device(d))

    def m_copy(d):
        return remote(mbuf.at[0], mbuf.at[d], ms.at[d], mr.at[d], device(d))

    def p_copy(d, other):
        return remote(pbuf.at[d], rbuf.at[d, other], ps.at[d, other], pr.at[d, other], device(d, other))

    lanes = pl.ds(pl.multiple_of((1 - t) * feats, feats), feats)
    base_copy = remote(base_ref.at[0, :, :, lanes], peer_base_ref, bs, br, device(0, 1))
    ends = [has_up, has_down]

    w_cross().start()
    for way in range(2):
        @pl.when(ends[way])
        def _(way=way):
            w_chain(way, z, 0, True).start()
            e_chain(way, z, True).start()
    for d in (1, 2, 3):
        m_copy(d).start()
        h_copy(d).start()
    for d in (2, 3):
        e_plane(d, z, True).start()
    base_copy.start()

    w_cross().wait_recv()
    for way in range(2):
        @pl.when(ends[way])
        def _(way=way):
            w_chain(way, z, 1).start()

    def shrink(zp, xr):
        number = (2 * zp + (1 - x if xr else x)).astype(jnp.float32)
        part = jnp.dot(
            hbuf[...].reshape(4 * rows, chunk), wbuf[zp, xr], preferred_element_type=jnp.float32
        ).reshape(4, rows, width)
        acc[...] = jnp.where(mbuf[...].astype(jnp.float32) == number, part, acc[...])

    def held(way, k):
        source = z - k if way == 0 else z + k
        exists = z >= k if way == 0 else z + k < nz
        return source, exists

    for k in range(1, nz):
        for xr in range(2):
            for way in range(2):
                source, exists = held(way, k)

                @pl.when(exists)
                def _(way=way, source=source, xr=xr, k=k):
                    w_chain(way, source, xr).wait_recv()

                @pl.when(jnp.logical_and(exists, ends[way]))
                def _(way=way, source=source, xr=xr, k=k):
                    w_chain(way, source, xr).start()

                if xr == 0:
                    @pl.when(exists)
                    def _(way=way, source=source):
                        e_chain(way, source).wait_recv()

                    @pl.when(jnp.logical_and(exists, ends[way]))
                    def _(way=way, source=source):
                        e_chain(way, source).start()

                    @pl.when(exists)
                    def _(way=way, source=source):
                        for d in (1, 2, 3):
                            e_plane(d, source).start()
                if k > 1:
                    @pl.when(exists)
                    def _(source=source, xr=xr):
                        shrink(source, xr)
        if k == 1:
            local_h.wait()
            local_w.wait()
            for d in (1, 2, 3):
                m_copy(d).wait_recv()
                h_copy(d).wait_recv()
            for xr in range(2):
                shrink(z, xr)
            for way in range(2):
                source, exists = held(way, k)

                @pl.when(exists)
                def _(source=source):
                    for xr in range(2):
                        shrink(source, xr)

    pbuf[...] = acc[...].astype(jnp.bfloat16)
    for d in (3, 2, 1, 0):
        for other in range(2):
            if d or other:
                p_copy(d, other).start()
    for copy in local_e:
        copy.wait()
    for way in range(2):
        for k in range(1, nz):
            source, exists = held(way, k)

            @pl.when(exists)
            def _(source=source):
                for d in (1, 2, 3):
                    e_plane(d, source).wait_recv()
    for d in (2, 3):
        e_plane(d, z, True).wait_recv()
    total = acc[0]
    for d in range(4):
        for other in range(2):
            if d or other:
                p_copy(d, other).wait_recv()
                total = total + rbuf[d, other].astype(jnp.float32)
    count = ebuf.shape[1] // rank
    total = total.astype(jnp.bfloat16)
    named = jnp.concatenate([mbuf[0].astype(jnp.float32)] * (count * rank // width), axis=1)
    chosen = named == (lax.broadcasted_iota(jnp.int32, (rows, count * rank), 1) // rank).astype(jnp.float32)
    for j in range(2):
        one = jnp.concatenate([total[:, j * rank:(j + 1) * rank]] * count, axis=1)
        spread = jnp.where(chosen, one.astype(jnp.float32), 0.0).astype(jnp.bfloat16)
        delta_ref[:, j, :] = jnp.dot(spread, ebuf[j], preferred_element_type=jnp.float32)

    base_copy.wait()
    w_cross().wait_send()
    for d in (1, 2, 3):
        m_copy(d).wait_send()
        h_copy(d).wait_send()
    for d in (2, 3):
        e_plane(d, z, True).wait_send()
    for d in range(4):
        for other in range(2):
            if d or other:
                p_copy(d, other).wait_send()
    for way in range(2):
        for k in range(nz):
            source, exists = held(way, k)

            @pl.when(jnp.logical_and(exists, ends[way]))
            def _(way=way, source=source, k=k):
                for xr in range(2):
                    w_chain(way, source, xr, k == 0).wait_send()
                e_chain(way, source, k == 0).wait_send()

            if k:
                @pl.when(exists)
                def _(source=source):
                    for d in (1, 2, 3):
                        e_plane(d, source).wait_send()


def local_planes(
    hidden, row_adapter_index, adapter_shrink_weight, adapter_expand_weight, base_partial_sums
):
    nz = lax.axis_size("adapter") // 2
    rows, width_here = hidden.shape
    chunk = width_here // 4
    width = adapter_shrink_weight.shape[2]
    rank, feats = adapter_expand_weight.shape[2:]
    dma = pltpu.SemaphoreType.DMA
    hbm = pl.BlockSpec(memory_space=pl.ANY)
    vmem = pl.BlockSpec(memory_space=pltpu.VMEM)
    bf16 = jnp.bfloat16
    delta, peer_base = pl.pallas_call(
        functools.partial(plane_kernel, nz),
        out_shape=(
            jax.ShapeDtypeStruct((rows, 2, feats), jnp.float32),
            jax.ShapeDtypeStruct((rows, 2, feats), bf16),
        ),
        in_specs=[hbm, vmem, hbm, hbm, hbm],
        out_specs=(vmem, hbm),
        scratch_shapes=[
            pltpu.VMEM((4, rows, chunk), bf16),
            pltpu.VMEM((4, rows, width), bf16),
            pltpu.VMEM((nz, 2, chunk, width), bf16),
            pltpu.VMEM((2, 2 * nz * rank, feats), bf16),
            pltpu.VMEM((4, rows, width), jnp.float32),
            pltpu.VMEM((4, rows, width), bf16),
            pltpu.VMEM((4, 2, rows, width), bf16),
            dma((4,)), dma((4,)), dma((4,)), dma((4,)),
            dma, dma, dma((2, nz, 2)), dma((nz, 2)),
            dma((2, nz)), dma((nz,)), dma((nz, 4)), dma((nz, 4)),
            dma((4, 2)), dma((4, 2)), dma, dma, dma((4,)),
        ],
        compiler_params=pltpu.CompilerParams(
            collective_id=0, has_side_effects=True, vmem_limit_bytes=60 * 1024 * 1024
        ),
    )(hidden, row_adapter_index.reshape(1, rows), adapter_shrink_weight, adapter_expand_weight, base_partial_sums)
    own = lax.dynamic_slice_in_dim(base_partial_sums[0], lax.axis_index("tensor") * feats, feats, axis=2)
    return (own.astype(jnp.float32) + peer_base.astype(jnp.float32) + delta).astype(bf16)


def local(
    hidden, row_adapter_index, adapter_shrink_weight, adapter_expand_weight, base_partial_sums
):
    row_count = hidden.shape[0]
    owner_count = lax.axis_size("adapter")
    capacity = max(2, (2 * row_count + owner_count - 1) // owner_count)
    slot_count = owner_count * capacity
    row_owner = row_adapter_index[:, 0]
    owner_hot = (row_owner[:, None] == jnp.arange(owner_count, dtype=jnp.int32)[None, :]).astype(
        jnp.float32
    )
    earlier = (jnp.arange(row_count)[:, None] > jnp.arange(row_count)[None, :]).astype(jnp.float32)
    before = jnp.dot(earlier, owner_hot, precision=lax.Precision.HIGHEST)
    slot_index = jnp.sum(before * owner_hot, axis=1)
    slot_hot = (slot_index[:, None] == jnp.arange(capacity, dtype=jnp.float32)[None, :]).astype(
        jnp.float32
    )
    placing = (owner_hot[:, :, None] * slot_hot[:, None, :]).reshape(row_count, slot_count)
    outgoing = jnp.dot(placing.T.astype(jnp.bfloat16), hidden, preferred_element_type=jnp.float32)
    outgoing = outgoing.astype(jnp.bfloat16).reshape(owner_count, capacity, hidden.shape[1])
    shrink_factor_table = adapter_shrink_weight[0]
    rank_index = adapter_expand_weight.shape[2]
    expand_factor_table = adapter_expand_weight[0].astype(jnp.float32)
    shrunk = lax.psum(
        jnp.einsum(
            "ocw,wk->ock",
            lax.all_to_all(outgoing, "adapter", split_axis=0, concat_axis=0, tiled=True),
            shrink_factor_table,
            preferred_element_type=jnp.float32,
        ),
        "tensor",
    )
    shrunk = shrunk.reshape(shrunk.shape[0], shrunk.shape[1], 2, rank_index)
    delta = jnp.einsum(
        "ocjk,jkf->ocjf", shrunk, expand_factor_table, precision=lax.Precision.HIGHEST
    )
    returned = lax.all_to_all(delta, "adapter", split_axis=0, concat_axis=0, tiled=True)
    row_delta = jnp.einsum(
        "rs,sjf->rjf",
        placing,
        returned.reshape(slot_count, 2, returned.shape[3]),
        precision=lax.Precision.HIGHEST,
    )
    base_sum = lax.psum_scatter(
        base_partial_sums[0].astype(jnp.float32).astype(jnp.bfloat16),
        "tensor",
        scatter_dimension=2,
        tiled=True,
    ).astype(jnp.float32)
    return (base_sum + row_delta).astype(jnp.bfloat16)


def solution(mesh):
    in_specs = (
        P(("groups", "adapter"), "tensor"),
        P(("groups", "adapter"), None),
        P("adapter", "tensor", None),
        P("adapter", None, None, "tensor"),
        P("tensor", ("groups", "adapter"), None, None),
    )
    out_specs = P(("groups", "adapter"), None, "tensor")
    adapters = mesh.shape["adapter"]
    planes = (
        mesh.shape["groups"] == 2 and mesh.shape["tensor"] == 2 and adapters % 2 == 0 and 4 <= adapters <= 16
    )
    step = local_planes if planes else local
    return jax.shard_map(step, mesh=mesh, in_specs=in_specs, out_specs=out_specs, check_vma=False)
```

```python
import functools

import jax
import jax.numpy as jnp
from jax import lax
from jax.experimental import pallas as pl
from jax.experimental.pallas import tpu as pltpu
from jax.sharding import PartitionSpec as P

MESH = pl.DeviceIdType.MESH
HI_EIGHTHS = 3


def plane_kernel(
    nz, hidden_ref, idx_ref, w_ref, e_ref, base_ref, delta_ref, peer_base_ref,
    hbuf, mbuf, wbuf, ebuf, acc, pbuf, rbuf, hbuf2, mbuf2, acc2, pbuf2, abuf,
    hs, hr, ms, mr, wxs, wxr, wzs, wzr, ezs, ezr, eps, epr, ps, pr, bs, br, ls, xs, xr_, as_, ar,
):
    y = lax.axis_index("groups")
    a = lax.axis_index("adapter")
    t = lax.axis_index("tensor")
    z = a // 2
    x = a % 2
    rows = hidden_ref.shape[0]
    chunk = hidden_ref.shape[1] // 4
    rank = e_ref.shape[2]
    feats = e_ref.shape[3]
    width = w_ref.shape[2]
    hi = hbuf2.shape[2]
    lo = chunk - hi
    last = nz - 1
    is_end = z % last == 0
    is_inner = z % last != 0
    by_end = jnp.logical_and(is_inner, (z - 1) % (last - 2) == 0)

    def coords(d):
        return (1 - x if d // 2 else x), (1 - y if d % 2 else y)

    def device(d, other=0):
        xx, yy = coords(d)
        return {"groups": yy, "adapter": 2 * z + xx, "tensor": 1 - t if other else t}

    def along(step):
        return {"groups": y, "adapter": 2 * (z + step) + x, "tensor": t}

    def quarter(d):
        xx, yy = coords(d)
        return pl.ds(pl.multiple_of((2 * xx + yy) * chunk, chunk), chunk)

    def remote(src, dst, send, recv, dev):
        return pltpu.make_async_remote_copy(
            src_ref=src, dst_ref=dst, send_sem=send, recv_sem=recv, device_id=dev, device_id_type=MESH
        )

    has_up = z < nz - 1
    has_down = z > 0
    barrier = pltpu.get_barrier_semaphore()
    for d in range(4):
        for other in range(2):
            if d or other:
                pl.semaphore_signal(barrier, inc=1, device_id=device(d, other), device_id_type=MESH)

    @pl.when(has_up)
    def _():
        pl.semaphore_signal(barrier, inc=1, device_id=along(1), device_id_type=MESH)

    @pl.when(has_down)
    def _():
        pl.semaphore_signal(barrier, inc=1, device_id=along(-1), device_id_type=MESH)

    local_h = pltpu.make_async_copy(hidden_ref.at[:, quarter(0)], hbuf.at[0], ls.at[0])
    local_w = pltpu.make_async_copy(w_ref.at[0, quarter(0)], wbuf.at[z, 0], ls.at[1])
    slot = pl.ds(pl.multiple_of(a * rank, rank), rank)
    local_e = [pltpu.make_async_copy(e_ref.at[0, j], ebuf.at[j, slot], ls.at[2 + j]) for j in range(2)]
    local_h.start()
    local_w.start()
    for copy in local_e:
        copy.start()
    mbuf[0] = jnp.broadcast_to(idx_ref[...].astype(jnp.float32), (width, rows)).T.astype(jnp.bfloat16)
    acc[...] = jnp.zeros_like(acc)
    pl.semaphore_wait(barrier, 7 + has_up.astype(jnp.int32) + has_down.astype(jnp.int32))

    def w_cross():
        return remote(w_ref.at[0, quarter(2)], wbuf.at[z, 1], wxs, wxr, device(2))

    def w_chain(way, zp, xr, size, own=False):
        here = wbuf.at[zp, xr, pl.ds(0, size)]
        src = w_ref.at[0, pl.ds(pl.multiple_of((2 * x + y) * chunk, chunk), size)] if own and xr == 0 else here
        return remote(src, here, wzs.at[way, zp, xr], wzr.at[zp, xr], along(1 - 2 * way))

    to_end = [z + 1 == last, z == 1]
    to_inner = [z + 1 != last, z != 1]

    def w_send(way, zp, xr, own=False):
        @pl.when(to_end[way])
        def _():
            w_chain(way, zp, xr, lo, own).start()

        @pl.when(to_inner[way])
        def _():
            w_chain(way, zp, xr, chunk, own).start()

    def w_sent(way, zp, xr, own=False):
        @pl.when(to_end[way])
        def _():
            w_chain(way, zp, xr, lo, own).wait_send()

        @pl.when(to_inner[way])
        def _():
            w_chain(way, zp, xr, chunk, own).wait_send()

    def w_arrived(way, zp, xr):
        @pl.when(is_end)
        def _():
            w_chain(way, zp, xr, lo).wait_recv()

        @pl.when(is_inner)
        def _():
            w_chain(way, zp, xr, chunk).wait_recv()

    inward = 1 - 2 * (z // last)
    outward = 2 * (z // (last - 1)) - 1

    def hi_copy(d):
        return remote(hbuf.at[d, :, pl.ds(lo, hi)], hbuf2.at[d], xs.at[d], xr_.at[d], along(inward))

    def m2_copy():
        return remote(mbuf, mbuf2, xs.at[4], xr_.at[4], along(inward))

    def a_copy():
        return remote(pbuf2, abuf, as_, ar, along(outward))

    def e_slot(zp):
        return ebuf.at[y, pl.ds(pl.multiple_of((2 * zp + x) * rank, rank), rank)]

    def e_chain(way, zp, own=False):
        src = e_ref.at[0, y] if own else e_slot(zp)
        return remote(src, e_slot(zp), ezs.at[way, zp], ezr.at[zp], along(1 - 2 * way))

    def e_plane(d, zp, own=False):
        src = e_ref.at[0, y] if own else e_slot(zp)
        return remote(src, e_slot(zp), eps.at[zp, d], epr.at[zp, d], device(d))

    def h_copy(d):
        return remote(hidden_ref.at[:, quarter(d)], hbuf.at[d], hs.at[d], hr.at[d], device(d))

    def m_copy(d):
        return remote(mbuf.at[0], mbuf.at[d], ms.at[d], mr.at[d], device(d))

    def p_copy(d, other):
        return remote(pbuf.at[d], rbuf.at[d, other], ps.at[d, other], pr.at[d, other], device(d, other))

    lanes = pl.ds(pl.multiple_of((1 - t) * feats, feats), feats)
    base_copy = remote(base_ref.at[0, :, :, lanes], peer_base_ref, bs, br, device(0, 1))
    ends = [has_up, has_down]

    w_cross().start()
    for way in range(2):
        @pl.when(ends[way])
        def _(way=way):
            w_send(way, z, 0, True)
    for d in (1, 2, 3):
        m_copy(d).start()
        h_copy(d).start()
    for d in (2, 3):
        e_plane(d, z, True).start()
    base_copy.start()

    w_cross().wait_recv()
    for way in range(2):
        @pl.when(ends[way])
        def _(way=way):
            w_send(way, z, 1)
            e_chain(way, z, True).start()

    local_h.wait()
    local_w.wait()

    @pl.when(is_end)
    def _():
        for d in (1, 2, 3):
            m_copy(d).wait_recv()
            h_copy(d).wait_recv()
        m2_copy().start()
        for d in range(4):
            hi_copy(d).start()

    def shrink(zp, xr):
        number = (2 * zp + (1 - x if xr else x)).astype(jnp.float32)
        names = mbuf[...].astype(jnp.float32) == number

        @pl.when(is_end)
        def _():
            part = jnp.dot(
                hbuf[:, :, :lo].reshape(4 * rows, lo), wbuf[zp, xr, :lo], preferred_element_type=jnp.float32
            ).reshape(4, rows, width)
            acc[...] = jnp.where(names, part, acc[...])

        @pl.when(is_inner)
        def _():
            part = jnp.dot(
                hbuf[...].reshape(4 * rows, chunk), wbuf[zp, xr], preferred_element_type=jnp.float32
            ).reshape(4, rows, width)
            acc[...] = jnp.where(names, part, acc[...])

    def held(way, k):
        source = z - k if way == 0 else z + k
        exists = z >= k if way == 0 else z + k < nz
        return source, exists

    for k in range(1, nz):
        for xr in range(2):
            for way in range(2):
                source, exists = held(way, k)

                @pl.when(exists)
                def _(way=way, source=source, xr=xr, k=k):
                    w_arrived(way, source, xr)

                @pl.when(jnp.logical_and(exists, ends[way]))
                def _(way=way, source=source, xr=xr, k=k):
                    w_send(way, source, xr)

                if xr == 1:
                    @pl.when(exists)
                    def _(way=way, source=source):
                        e_chain(way, source).wait_recv()

                    @pl.when(jnp.logical_and(exists, ends[way]))
                    def _(way=way, source=source):
                        e_chain(way, source).start()

                    @pl.when(exists)
                    def _(way=way, source=source):
                        for d in (1, 2, 3):
                            e_plane(d, source).start()
                if k > 1:
                    @pl.when(exists)
                    def _(source=source, xr=xr):
                        shrink(source, xr)
        if k == 1:
            @pl.when(is_inner)
            def _():
                for d in (1, 2, 3):
                    m_copy(d).wait_recv()
                    h_copy(d).wait_recv()
            for xr in range(2):
                shrink(z, xr)
            for way in range(2):
                source, exists = held(way, k)

                @pl.when(exists)
                def _(source=source):
                    for xr in range(2):
                        shrink(source, xr)

    @pl.when(is_end)
    def _():
        a_copy().wait_recv()
        acc[...] += abuf[...].astype(jnp.float32)

    pbuf[...] = acc[...].astype(jnp.bfloat16)
    for d in (3, 2, 1, 0):
        for other in range(2):
            if d or other:
                p_copy(d, other).start()

    @pl.when(by_end)
    def _():
        m2_copy().wait_recv()
        for d in range(4):
            hi_copy(d).wait_recv()
        acc2[...] = jnp.zeros_like(acc2)

        def one(i, carry):
            zp, xr = i // 2, i % 2
            number = (2 * zp + (x + xr) % 2).astype(jnp.float32)
            part = jnp.dot(
                hbuf2[...].reshape(4 * rows, hi), wbuf[zp, xr, lo:], preferred_element_type=jnp.float32
            ).reshape(4, rows, width)
            acc2[...] = jnp.where(mbuf2[...].astype(jnp.float32) == number, part, acc2[...])
            return carry

        lax.fori_loop(0, 2 * nz, one, 0)
        pbuf2[...] = acc2[...].astype(jnp.bfloat16)
        a_copy().start()

    for copy in local_e:
        copy.wait()
    for way in range(2):
        for k in range(1, nz):
            source, exists = held(way, k)

            @pl.when(exists)
            def _(source=source):
                for d in (1, 2, 3):
                    e_plane(d, source).wait_recv()
    for d in (2, 3):
        e_plane(d, z, True).wait_recv()
    total = acc[0]
    for d in range(4):
        for other in range(2):
            if d or other:
                p_copy(d, other).wait_recv()
                total = total + rbuf[d, other].astype(jnp.float32)
    count = ebuf.shape[1] // rank
    total = total.astype(jnp.bfloat16)
    named = jnp.concatenate([mbuf[0].astype(jnp.float32)] * (count * rank // width), axis=1)
    chosen = named == (lax.broadcasted_iota(jnp.int32, (rows, count * rank), 1) // rank).astype(jnp.float32)
    for j in range(2):
        one = jnp.concatenate([total[:, j * rank:(j + 1) * rank]] * count, axis=1)
        spread = jnp.where(chosen, one.astype(jnp.float32), 0.0).astype(jnp.bfloat16)
        delta_ref[:, j, :] = jnp.dot(spread, ebuf[j], preferred_element_type=jnp.float32)

    @pl.when(is_end)
    def _():
        m2_copy().wait_send()
        for d in range(4):
            hi_copy(d).wait_send()

    @pl.when(by_end)
    def _():
        a_copy().wait_send()

    base_copy.wait()
    w_cross().wait_send()
    for d in (1, 2, 3):
        m_copy(d).wait_send()
        h_copy(d).wait_send()
    for d in (2, 3):
        e_plane(d, z, True).wait_send()
    for d in range(4):
        for other in range(2):
            if d or other:
                p_copy(d, other).wait_send()
    for way in range(2):
        for k in range(nz):
            source, exists = held(way, k)

            @pl.when(jnp.logical_and(exists, ends[way]))
            def _(way=way, source=source, k=k):
                for xr in range(2):
                    w_sent(way, source, xr, k == 0)
                e_chain(way, source, k == 0).wait_send()

            if k:
                @pl.when(exists)
                def _(source=source):
                    for d in (1, 2, 3):
                        e_plane(d, source).wait_send()


def local_planes(
    hidden, row_adapter_index, adapter_shrink_weight, adapter_expand_weight, base_partial_sums
):
    nz = lax.axis_size("adapter") // 2
    rows, width_here = hidden.shape
    chunk = width_here // 4
    hi = chunk * HI_EIGHTHS // 8
    width = adapter_shrink_weight.shape[2]
    rank, feats = adapter_expand_weight.shape[2:]
    dma = pltpu.SemaphoreType.DMA
    hbm = pl.BlockSpec(memory_space=pl.ANY)
    vmem = pl.BlockSpec(memory_space=pltpu.VMEM)
    bf16 = jnp.bfloat16
    delta, peer_base = pl.pallas_call(
        functools.partial(plane_kernel, nz),
        out_shape=(
            jax.ShapeDtypeStruct((rows, 2, feats), jnp.float32),
            jax.ShapeDtypeStruct((rows, 2, feats), bf16),
        ),
        in_specs=[hbm, vmem, hbm, hbm, hbm],
        out_specs=(vmem, hbm),
        scratch_shapes=[
            pltpu.VMEM((4, rows, chunk), bf16),
            pltpu.VMEM((4, rows, width), bf16),
            pltpu.VMEM((nz, 2, chunk, width), bf16),
            pltpu.VMEM((2, 2 * nz * rank, feats), bf16),
            pltpu.VMEM((4, rows, width), jnp.float32),
            pltpu.VMEM((4, rows, width), bf16),
            pltpu.VMEM((4, 2, rows, width), bf16),
            pltpu.VMEM((4, rows, hi), bf16),
            pltpu.VMEM((4, rows, width), bf16),
            pltpu.VMEM((4, rows, width), jnp.float32),
            pltpu.VMEM((4, rows, width), bf16),
            pltpu.VMEM((4, rows, width), bf16),
            dma((4,)), dma((4,)), dma((4,)), dma((4,)),
            dma, dma, dma((2, nz, 2)), dma((nz, 2)),
            dma((2, nz)), dma((nz,)), dma((nz, 4)), dma((nz, 4)),
            dma((4, 2)), dma((4, 2)), dma, dma, dma((4,)),
            dma((5,)), dma((5,)), dma, dma,
        ],
        compiler_params=pltpu.CompilerParams(
            collective_id=0, has_side_effects=True, vmem_limit_bytes=60 * 1024 * 1024
        ),
    )(hidden, row_adapter_index.reshape(1, rows), adapter_shrink_weight, adapter_expand_weight, base_partial_sums)
    own = lax.dynamic_slice_in_dim(base_partial_sums[0], lax.axis_index("tensor") * feats, feats, axis=2)
    return (own.astype(jnp.float32) + peer_base.astype(jnp.float32) + delta).astype(bf16)


def local(
    hidden, row_adapter_index, adapter_shrink_weight, adapter_expand_weight, base_partial_sums
):
    row_count = hidden.shape[0]
    owner_count = lax.axis_size("adapter")
    capacity = max(2, (2 * row_count + owner_count - 1) // owner_count)
    slot_count = owner_count * capacity
    row_owner = row_adapter_index[:, 0]
    owner_hot = (row_owner[:, None] == jnp.arange(owner_count, dtype=jnp.int32)[None, :]).astype(
        jnp.float32
    )
    earlier = (jnp.arange(row_count)[:, None] > jnp.arange(row_count)[None, :]).astype(jnp.float32)
    before = jnp.dot(earlier, owner_hot, precision=lax.Precision.HIGHEST)
    slot_index = jnp.sum(before * owner_hot, axis=1)
    slot_hot = (slot_index[:, None] == jnp.arange(capacity, dtype=jnp.float32)[None, :]).astype(
        jnp.float32
    )
    placing = (owner_hot[:, :, None] * slot_hot[:, None, :]).reshape(row_count, slot_count)
    outgoing = jnp.dot(placing.T.astype(jnp.bfloat16), hidden, preferred_element_type=jnp.float32)
    outgoing = outgoing.astype(jnp.bfloat16).reshape(owner_count, capacity, hidden.shape[1])
    shrink_factor_table = adapter_shrink_weight[0]
    rank_index = adapter_expand_weight.shape[2]
    expand_factor_table = adapter_expand_weight[0].astype(jnp.float32)
    shrunk = lax.psum(
        jnp.einsum(
            "ocw,wk->ock",
            lax.all_to_all(outgoing, "adapter", split_axis=0, concat_axis=0, tiled=True),
            shrink_factor_table,
            preferred_element_type=jnp.float32,
        ),
        "tensor",
    )
    shrunk = shrunk.reshape(shrunk.shape[0], shrunk.shape[1], 2, rank_index)
    delta = jnp.einsum(
        "ocjk,jkf->ocjf", shrunk, expand_factor_table, precision=lax.Precision.HIGHEST
    )
    returned = lax.all_to_all(delta, "adapter", split_axis=0, concat_axis=0, tiled=True)
    row_delta = jnp.einsum(
        "rs,sjf->rjf",
        placing,
        returned.reshape(slot_count, 2, returned.shape[3]),
        precision=lax.Precision.HIGHEST,
    )
    base_sum = lax.psum_scatter(
        base_partial_sums[0].astype(jnp.float32).astype(jnp.bfloat16),
        "tensor",
        scatter_dimension=2,
        tiled=True,
    ).astype(jnp.float32)
    return (base_sum + row_delta).astype(jnp.bfloat16)


def solution(mesh):
    in_specs = (
        P(("groups", "adapter"), "tensor"),
        P(("groups", "adapter"), None),
        P("adapter", "tensor", None),
        P("adapter", None, None, "tensor"),
        P("tensor", ("groups", "adapter"), None, None),
    )
    out_specs = P(("groups", "adapter"), None, "tensor")
    adapters = mesh.shape["adapter"]
    planes = (
        mesh.shape["groups"] == 2 and mesh.shape["tensor"] == 2 and adapters % 2 == 0 and 8 <= adapters <= 16
    )
    step = local_planes if planes else local
    return jax.shard_map(step, mesh=mesh, in_specs=in_specs, out_specs=out_specs, check_vma=False)
```

```python
import functools

import jax
import jax.numpy as jnp
from jax import lax
from jax.experimental import pallas as pl
from jax.experimental.pallas import tpu as pltpu
from jax.sharding import PartitionSpec as P

MESH = pl.DeviceIdType.MESH
HI_EIGHTHS = 3


def plane_kernel(
    nz, hidden_ref, idx_ref, w_ref, e_ref, base_ref, delta_ref, peer_base_ref,
    hbuf, mbuf, wbuf, ebuf, acc, pbuf, rbuf, hbuf2, mbuf2, acc2, pbuf2, abuf,
    hs, hr, ms, mr, wxs, wxr, wzs, wzr, ezs, ezr, eps, epr, ps, pr, bs, br, ls, xs, xr_, as_, ar,
):
    y = lax.axis_index("groups")
    a = lax.axis_index("adapter")
    t = lax.axis_index("tensor")
    z = a // 2
    x = a % 2
    rows = hidden_ref.shape[0]
    chunk = hidden_ref.shape[1] // 4
    rank = e_ref.shape[2]
    feats = e_ref.shape[3]
    width = w_ref.shape[2]
    hi = hbuf2.shape[2]
    lo = chunk - hi
    last = nz - 1
    is_end = z % last == 0
    is_inner = z % last != 0
    inward = 1 - 2 * (z // last)
    outward = 2 * (z // (last - 1)) - 1

    def coords(d):
        return (1 - x if d // 2 else x), (1 - y if d % 2 else y)

    def device(d, other=0):
        xx, yy = coords(d)
        return {"groups": yy, "adapter": 2 * z + xx, "tensor": 1 - t if other else t}

    def along(step):
        return {"groups": y, "adapter": 2 * (z + step) + x, "tensor": t}

    def quarter(d):
        xx, yy = coords(d)
        return pl.ds(pl.multiple_of((2 * xx + yy) * chunk, chunk), chunk)

    def remote(src, dst, send, recv, dev):
        return pltpu.make_async_remote_copy(
            src_ref=src, dst_ref=dst, send_sem=send, recv_sem=recv, device_id=dev, device_id_type=MESH
        )

    has_up = z < nz - 1
    has_down = z > 0
    barrier = pltpu.get_barrier_semaphore()
    for d in range(4):
        for other in range(2):
            if d or other:
                pl.semaphore_signal(barrier, inc=1, device_id=device(d, other), device_id_type=MESH)

    @pl.when(has_up)
    def _():
        pl.semaphore_signal(barrier, inc=1, device_id=along(1), device_id_type=MESH)

    @pl.when(has_down)
    def _():
        pl.semaphore_signal(barrier, inc=1, device_id=along(-1), device_id_type=MESH)

    local_h = pltpu.make_async_copy(hidden_ref.at[:, quarter(0)], hbuf.at[0], ls.at[0])
    local_w = pltpu.make_async_copy(w_ref.at[0, quarter(0)], wbuf.at[z, 0], ls.at[1])
    slot = pl.ds(pl.multiple_of(a * rank, rank), rank)
    local_e = [pltpu.make_async_copy(e_ref.at[0, j], ebuf.at[j, slot], ls.at[2 + j]) for j in range(2)]
    local_h.start()
    local_w.start()
    for copy in local_e:
        copy.start()
    mbuf[0] = jnp.broadcast_to(idx_ref[...].astype(jnp.float32), (width, rows)).T.astype(jnp.bfloat16)
    acc[...] = jnp.zeros_like(acc)
    pl.semaphore_wait(barrier, 7 + has_up.astype(jnp.int32) + has_down.astype(jnp.int32))

    def w_cross():
        return remote(w_ref.at[0, quarter(2)], wbuf.at[z, 1], wxs, wxr, device(2))

    def w_copy(step, way, zp, xr, size, own=False):
        here = wbuf.at[zp, xr, pl.ds(0, size)]
        src = w_ref.at[0, pl.ds(pl.multiple_of((2 * x + y) * chunk, chunk), size)] if own else here
        return remote(src, here, wzs.at[way, zp, xr], wzr.at[zp, xr], along(step))

    def w_out(zp, xr, own=False):
        return w_copy(outward, 0, zp, xr, lo, own)

    def w_across(zp, xr, own=False):
        return w_copy(-outward, 1, zp, xr, chunk, own)

    def w_in(zp, xr, own=False):
        return w_copy(inward, 0, zp, xr, chunk, own)

    def w_got(zp, xr):
        return w_copy(inward, 0, zp, xr, lo)

    def hi_copy(d):
        return remote(hbuf.at[d, :, pl.ds(lo, hi)], hbuf2.at[d], xs.at[d], xr_.at[d], along(inward))

    def m2_copy():
        return remote(mbuf, mbuf2, xs.at[4], xr_.at[4], along(inward))

    def a_copy():
        return remote(pbuf2, abuf, as_, ar, along(outward))

    def e_slot(zp):
        return ebuf.at[y, pl.ds(pl.multiple_of((2 * zp + x) * rank, rank), rank)]

    def e_chain(step, way, zp, own=False):
        src = e_ref.at[0, y] if own else e_slot(zp)
        return remote(src, e_slot(zp), ezs.at[way, zp], ezr.at[zp], along(step))

    def e_plane(d, zp, own=False):
        src = e_ref.at[0, y] if own else e_slot(zp)
        return remote(src, e_slot(zp), eps.at[zp, d], epr.at[zp, d], device(d))

    def h_copy(d):
        return remote(hidden_ref.at[:, quarter(d)], hbuf.at[d], hs.at[d], hr.at[d], device(d))

    def m_copy(d):
        return remote(mbuf.at[0], mbuf.at[d], ms.at[d], mr.at[d], device(d))

    def p_copy(d, other):
        return remote(pbuf.at[d], rbuf.at[d, other], ps.at[d, other], pr.at[d, other], device(d, other))

    lanes = pl.ds(pl.multiple_of((1 - t) * feats, feats), feats)
    base_copy = remote(base_ref.at[0, :, :, lanes], peer_base_ref, bs, br, device(0, 1))

    w_cross().start()
    for d in (1, 2, 3):
        m_copy(d).start()
    h_copy(1).start()

    @pl.when(is_inner)
    def _():
        w_out(z, 0, True).start()
        w_across(z, 0, True).start()

    @pl.when(is_end)
    def _():
        w_in(z, 0, True).start()

    base_copy.start()
    local_h.wait()
    local_w.wait()
    w_cross().wait_recv()
    for d in (2, 3):
        h_copy(d).start()

    def spread(zp):
        e_chain(inward, 0, zp).wait_recv()
        for d in (1, 2, 3):
            e_plane(d, zp).start()

    def send_partials():
        pbuf[...] = acc[...].astype(jnp.bfloat16)
        for d in (3, 2, 1, 0):
            for other in range(2):
                if d or other:
                    p_copy(d, other).start()

    def shrink(zp, xr, size):
        number = (2 * zp + (1 - x if xr else x)).astype(jnp.float32)
        part = jnp.dot(
            hbuf[:, :, :size].reshape(4 * rows, size), wbuf[zp, xr, :size], preferred_element_type=jnp.float32
        ).reshape(4, rows, width)
        acc[...] = jnp.where(mbuf[...].astype(jnp.float32) == number, part, acc[...])

    def shrink_end(zp, xr):
        number = (2 * zp + (x + xr) % 2).astype(jnp.float32)
        part = jnp.dot(
            hbuf2[...].reshape(4 * rows, hi), wbuf[zp, xr, lo:], preferred_element_type=jnp.float32
        ).reshape(4, rows, width)
        acc2[...] = jnp.where(mbuf2[...].astype(jnp.float32) == number, part, acc2[...])

    @pl.when(is_inner)
    def _():
        zn, zo = z + outward, last - z
        zf = last - zn
        w_out(z, 0, True).wait_send()
        w_out(z, 1).start()
        w_across(zn, 0).wait_recv()
        w_across(z, 0, True).wait_send()
        w_across(zn, 0).start()
        w_across(zo, 0).wait_recv()
        w_out(z, 1).wait_send()
        e_chain(outward, 0, z, True).start()
        w_out(zo, 0).start()
        w_across(zn, 1).wait_recv()
        w_across(zn, 0).wait_send()
        w_across(zn, 1).start()
        for d in (2, 3):
            e_plane(d, z, True).start()
        acc2[...] = jnp.zeros_like(acc2)
        w_across(zf, 0).wait_recv()
        w_out(zo, 0).wait_send()
        w_out(zf, 0).start()
        spread(zn)
        w_across(zn, 1).wait_send()
        e_chain(-outward, 1, zn).start()
        w_across(z, 1).start()
        for d in (1, 2, 3):
            m_copy(d).wait_recv()
            h_copy(d).wait_recv()
        for zp, xr in ((z, 0), (z, 1), (zn, 0), (zn, 1), (zo, 0), (zf, 0)):
            shrink(zp, xr, chunk)
        w_across(zf, 1).wait_recv()
        w_out(zf, 0).wait_send()
        w_out(zf, 1).start()
        shrink(zf, 1, chunk)
        m2_copy().wait_recv()
        for d in range(4):
            hi_copy(d).wait_recv()

        lax.fori_loop(0, nz, lambda i, c: (shrink_end(i, 0), c)[1], 0)
        lax.fori_loop(1, nz, lambda i, c: (shrink_end((zo + i) % nz, 1), c)[1], 0)
        spread(zf)
        e_chain(outward, 0, zf).start()
        w_across(z, 1).wait_send()
        e_chain(-outward, 1, z, True).start()
        w_across(zo, 1).wait_recv()
        w_out(zf, 1).wait_send()
        w_out(zo, 1).start()
        shrink_end(zo, 1)
        pbuf2[...] = acc2[...].astype(jnp.bfloat16)
        a_copy().start()
        shrink(zo, 1, chunk)
        send_partials()
        spread(zo)
        e_chain(outward, 0, zo).start()

    @pl.when(is_end)
    def _():
        zi, zf = z + inward, last - z
        zo = last - zi
        w_in(z, 0, True).wait_send()
        w_in(z, 1).start()
        w_in(z, 1).wait_send()
        e_chain(inward, 0, z, True).start()
        hi_copy(0).start()
        h_copy(1).wait_recv()
        hi_copy(1).start()
        for d in (2, 3):
            e_plane(d, z, True).start()
        for d in (1, 2, 3):
            m_copy(d).wait_recv()
        m2_copy().start()
        for d in (2, 3):
            h_copy(d).wait_recv()
            hi_copy(d).start()
        shrink(z, 0, lo)
        shrink(z, 1, lo)
        for xr in range(2):
            w_got(zi, xr).wait_recv()
            shrink(zi, xr, lo)
        spread(zi)
        for zp, xr in ((zo, 0), (zf, 0), (zf, 1)):
            w_got(zp, xr).wait_recv()
            shrink(zp, xr, lo)
        spread(zf)
        w_got(zo, 1).wait_recv()
        shrink(zo, 1, lo)
        a_copy().wait_recv()
        acc[...] += abuf[...].astype(jnp.float32)
        send_partials()
        spread(zo)

    for copy in local_e:
        copy.wait()
    for k in range(1, nz):
        for d in (1, 2, 3):
            e_plane(d, (z + k) % nz).wait_recv()
    for d in (2, 3):
        e_plane(d, z, True).wait_recv()
    total = acc[0]
    for d in range(4):
        for other in range(2):
            if d or other:
                p_copy(d, other).wait_recv()
                total = total + rbuf[d, other].astype(jnp.float32)
    count = ebuf.shape[1] // rank
    total = total.astype(jnp.bfloat16)
    named = jnp.concatenate([mbuf[0].astype(jnp.float32)] * (count * rank // width), axis=1)
    chosen = named == (lax.broadcasted_iota(jnp.int32, (rows, count * rank), 1) // rank).astype(jnp.float32)
    for j in range(2):
        one = jnp.concatenate([total[:, j * rank:(j + 1) * rank]] * count, axis=1)
        spread = jnp.where(chosen, one.astype(jnp.float32), 0.0).astype(jnp.bfloat16)
        delta_ref[:, j, :] = jnp.dot(spread, ebuf[j], preferred_element_type=jnp.float32)

    @pl.when(is_end)
    def _():
        m2_copy().wait_send()
        for d in range(4):
            hi_copy(d).wait_send()
        e_chain(inward, 0, z, True).wait_send()

    @pl.when(is_inner)
    def _():
        zn, zo = z + outward, last - z
        zf = last - zn
        a_copy().wait_send()
        w_out(zo, 1).wait_send()
        for zp in (zo, zf):
            e_chain(outward, 0, zp).wait_send()
        e_chain(outward, 0, z, True).wait_send()
        e_chain(-outward, 1, zn).wait_send()
        e_chain(-outward, 1, z, True).wait_send()

    base_copy.wait()
    w_cross().wait_send()
    for d in (1, 2, 3):
        m_copy(d).wait_send()
        h_copy(d).wait_send()
    for d in (2, 3):
        e_plane(d, z, True).wait_send()
    for d in range(4):
        for other in range(2):
            if d or other:
                p_copy(d, other).wait_send()
    for k in range(1, nz):
        for d in (1, 2, 3):
            e_plane(d, (z + k) % nz).wait_send()


def local_planes(
    hidden, row_adapter_index, adapter_shrink_weight, adapter_expand_weight, base_partial_sums
):
    nz = lax.axis_size("adapter") // 2
    rows, width_here = hidden.shape
    chunk = width_here // 4
    hi = chunk * HI_EIGHTHS // 8
    width = adapter_shrink_weight.shape[2]
    rank, feats = adapter_expand_weight.shape[2:]
    dma = pltpu.SemaphoreType.DMA
    hbm = pl.BlockSpec(memory_space=pl.ANY)
    vmem = pl.BlockSpec(memory_space=pltpu.VMEM)
    bf16 = jnp.bfloat16
    delta, peer_base = pl.pallas_call(
        functools.partial(plane_kernel, nz),
        out_shape=(
            jax.ShapeDtypeStruct((rows, 2, feats), jnp.float32),
            jax.ShapeDtypeStruct((rows, 2, feats), bf16),
        ),
        in_specs=[hbm, vmem, hbm, hbm, hbm],
        out_specs=(vmem, hbm),
        scratch_shapes=[
            pltpu.VMEM((4, rows, chunk), bf16),
            pltpu.VMEM((4, rows, width), bf16),
            pltpu.VMEM((nz, 2, chunk, width), bf16),
            pltpu.VMEM((2, 2 * nz * rank, feats), bf16),
            pltpu.VMEM((4, rows, width), jnp.float32),
            pltpu.VMEM((4, rows, width), bf16),
            pltpu.VMEM((4, 2, rows, width), bf16),
            pltpu.VMEM((4, rows, hi), bf16),
            pltpu.VMEM((4, rows, width), bf16),
            pltpu.VMEM((4, rows, width), jnp.float32),
            pltpu.VMEM((4, rows, width), bf16),
            pltpu.VMEM((4, rows, width), bf16),
            dma((4,)), dma((4,)), dma((4,)), dma((4,)),
            dma, dma, dma((2, nz, 2)), dma((nz, 2)),
            dma((2, nz)), dma((nz,)), dma((nz, 4)), dma((nz, 4)),
            dma((4, 2)), dma((4, 2)), dma, dma, dma((4,)),
            dma((5,)), dma((5,)), dma, dma,
        ],
        compiler_params=pltpu.CompilerParams(
            collective_id=0, has_side_effects=True, vmem_limit_bytes=60 * 1024 * 1024
        ),
    )(hidden, row_adapter_index.reshape(1, rows), adapter_shrink_weight, adapter_expand_weight, base_partial_sums)
    own = lax.dynamic_slice_in_dim(base_partial_sums[0], lax.axis_index("tensor") * feats, feats, axis=2)
    return (own.astype(jnp.float32) + peer_base.astype(jnp.float32) + delta).astype(bf16)


def local(
    hidden, row_adapter_index, adapter_shrink_weight, adapter_expand_weight, base_partial_sums
):
    row_count = hidden.shape[0]
    owner_count = lax.axis_size("adapter")
    capacity = max(2, (2 * row_count + owner_count - 1) // owner_count)
    slot_count = owner_count * capacity
    row_owner = row_adapter_index[:, 0]
    owner_hot = (row_owner[:, None] == jnp.arange(owner_count, dtype=jnp.int32)[None, :]).astype(
        jnp.float32
    )
    earlier = (jnp.arange(row_count)[:, None] > jnp.arange(row_count)[None, :]).astype(jnp.float32)
    before = jnp.dot(earlier, owner_hot, precision=lax.Precision.HIGHEST)
    slot_index = jnp.sum(before * owner_hot, axis=1)
    slot_hot = (slot_index[:, None] == jnp.arange(capacity, dtype=jnp.float32)[None, :]).astype(
        jnp.float32
    )
    placing = (owner_hot[:, :, None] * slot_hot[:, None, :]).reshape(row_count, slot_count)
    outgoing = jnp.dot(placing.T.astype(jnp.bfloat16), hidden, preferred_element_type=jnp.float32)
    outgoing = outgoing.astype(jnp.bfloat16).reshape(owner_count, capacity, hidden.shape[1])
    shrink_factor_table = adapter_shrink_weight[0]
    rank_index = adapter_expand_weight.shape[2]
    expand_factor_table = adapter_expand_weight[0].astype(jnp.float32)
    shrunk = lax.psum(
        jnp.einsum(
            "ocw,wk->ock",
            lax.all_to_all(outgoing, "adapter", split_axis=0, concat_axis=0, tiled=True),
            shrink_factor_table,
            preferred_element_type=jnp.float32,
        ),
        "tensor",
    )
    shrunk = shrunk.reshape(shrunk.shape[0], shrunk.shape[1], 2, rank_index)
    delta = jnp.einsum(
        "ocjk,jkf->ocjf", shrunk, expand_factor_table, precision=lax.Precision.HIGHEST
    )
    returned = lax.all_to_all(delta, "adapter", split_axis=0, concat_axis=0, tiled=True)
    row_delta = jnp.einsum(
        "rs,sjf->rjf",
        placing,
        returned.reshape(slot_count, 2, returned.shape[3]),
        precision=lax.Precision.HIGHEST,
    )
    base_sum = lax.psum_scatter(
        base_partial_sums[0].astype(jnp.float32).astype(jnp.bfloat16),
        "tensor",
        scatter_dimension=2,
        tiled=True,
    ).astype(jnp.float32)
    return (base_sum + row_delta).astype(jnp.bfloat16)


def solution(mesh):
    in_specs = (
        P(("groups", "adapter"), "tensor"),
        P(("groups", "adapter"), None),
        P("adapter", "tensor", None),
        P("adapter", None, None, "tensor"),
        P("tensor", ("groups", "adapter"), None, None),
    )
    out_specs = P(("groups", "adapter"), None, "tensor")
    adapters = mesh.shape["adapter"]
    planes = (
        mesh.shape["groups"] == 2 and mesh.shape["tensor"] == 2 and adapters == 8
    )
    step = local_planes if planes else local
    return jax.shard_map(step, mesh=mesh, in_specs=in_specs, out_specs=out_specs, check_vma=False)
```

```python
import functools

import jax
import jax.numpy as jnp
from jax import lax
from jax.experimental import pallas as pl
from jax.experimental.pallas import tpu as pltpu
from jax.sharding import PartitionSpec as P

MESH = pl.DeviceIdType.MESH
HI_EIGHTHS = 3


def plane_kernel(
    nz, hidden_ref, idx_ref, w_ref, e_ref, base_ref, delta_ref, peer_base_ref,
    hbuf, mbuf, wbuf, ebuf, acc, pbuf, rbuf, hbuf2, mbuf2, acc2, pbuf2, abuf,
    hs, hr, ms, mr, wxs, wxr, wzs, wzr, ezs, ezr, eps, epr, ps, pr, bs, br, ls, xs, xr_, as_, ar,
):
    y = lax.axis_index("groups")
    a = lax.axis_index("adapter")
    t = lax.axis_index("tensor")
    z = a // 2
    x = a % 2
    rows = hidden_ref.shape[0]
    chunk = hidden_ref.shape[1] // 4
    rank = e_ref.shape[2]
    feats = e_ref.shape[3]
    width = w_ref.shape[2]
    hi = hbuf2.shape[2]
    lo = chunk - hi
    last = nz - 1
    is_end = z % last == 0
    is_inner = z % last != 0
    inward = 1 - 2 * (z // last)
    outward = 2 * (z // (last - 1)) - 1

    def coords(d):
        return (1 - x if d // 2 else x), (1 - y if d % 2 else y)

    def device(d, other=0):
        xx, yy = coords(d)
        return {"groups": yy, "adapter": 2 * z + xx, "tensor": 1 - t if other else t}

    def along(step):
        return {"groups": y, "adapter": 2 * (z + step) + x, "tensor": t}

    def quarter(d):
        xx, yy = coords(d)
        return pl.ds(pl.multiple_of((2 * xx + yy) * chunk, chunk), chunk)

    def remote(src, dst, send, recv, dev):
        return pltpu.make_async_remote_copy(
            src_ref=src, dst_ref=dst, send_sem=send, recv_sem=recv, device_id=dev, device_id_type=MESH
        )

    has_up = z < nz - 1
    has_down = z > 0
    barrier = pltpu.get_barrier_semaphore()
    for d in range(4):
        for other in range(2):
            if d or other:
                pl.semaphore_signal(barrier, inc=1, device_id=device(d, other), device_id_type=MESH)

    @pl.when(has_up)
    def _():
        pl.semaphore_signal(barrier, inc=1, device_id=along(1), device_id_type=MESH)

    @pl.when(has_down)
    def _():
        pl.semaphore_signal(barrier, inc=1, device_id=along(-1), device_id_type=MESH)

    local_h = pltpu.make_async_copy(hidden_ref.at[:, quarter(0)], hbuf.at[0], ls.at[0])
    local_w = pltpu.make_async_copy(w_ref.at[0, quarter(0)], wbuf.at[z, 0], ls.at[1])
    slot = pl.ds(pl.multiple_of(a * rank, rank), rank)
    local_e = [pltpu.make_async_copy(e_ref.at[0, j], ebuf.at[j, slot], ls.at[2 + j]) for j in range(2)]
    local_h.start()
    local_w.start()
    for copy in local_e:
        copy.start()
    mbuf[0] = jnp.broadcast_to(idx_ref[...].astype(jnp.float32), (width, rows)).T.astype(jnp.bfloat16)
    acc[...] = jnp.zeros_like(acc)
    pl.semaphore_wait(barrier, 7 + has_up.astype(jnp.int32) + has_down.astype(jnp.int32))

    def w_cross():
        return remote(w_ref.at[0, quarter(2)], wbuf.at[z, 1], wxs, wxr, device(2))

    def w_copy(step, way, zp, xr, size, own=False):
        here = wbuf.at[zp, xr, pl.ds(0, size)]
        src = w_ref.at[0, pl.ds(pl.multiple_of((2 * x + y) * chunk, chunk), size)] if own else here
        return remote(src, here, wzs.at[way, zp, xr], wzr.at[zp, xr], along(step))

    def w_out(zp, xr, own=False):
        return w_copy(outward, 0, zp, xr, lo, own)

    def w_across(zp, xr, own=False):
        return w_copy(-outward, 1, zp, xr, chunk, own)

    def w_in(zp, xr, own=False):
        return w_copy(inward, 0, zp, xr, chunk, own)

    def w_got(zp, xr):
        return w_copy(inward, 0, zp, xr, lo)

    def hi_copy(d):
        return remote(hbuf.at[d, :, pl.ds(lo, hi)], hbuf2.at[d], xs.at[d], xr_.at[d], along(inward))

    def m2_copy():
        return remote(mbuf, mbuf2, xs.at[4], xr_.at[4], along(inward))

    def a_copy():
        return remote(pbuf2, abuf, as_, ar, along(outward))

    def e_slot(zp):
        return ebuf.at[y, pl.ds(pl.multiple_of((2 * zp + x) * rank, rank), rank)]

    def e_chain(step, way, zp, own=False):
        src = e_ref.at[0, y] if own else e_slot(zp)
        return remote(src, e_slot(zp), ezs.at[way, zp], ezr.at[zp], along(step))

    def e_plane(d, zp, own=False):
        src = e_ref.at[0, y] if own else e_slot(zp)
        return remote(src, e_slot(zp), eps.at[zp, d], epr.at[zp, d], device(d))

    def h_copy(d):
        return remote(hidden_ref.at[:, quarter(d)], hbuf.at[d], hs.at[d], hr.at[d], device(d))

    def m_copy(d):
        return remote(mbuf.at[0], mbuf.at[d], ms.at[d], mr.at[d], device(d))

    def p_copy(d, other):
        return remote(pbuf.at[d], rbuf.at[d, other], ps.at[d, other], pr.at[d, other], device(d, other))

    lanes = pl.ds(pl.multiple_of((1 - t) * feats, feats), feats)
    base_copy = remote(base_ref.at[0, :, :, lanes], peer_base_ref, bs, br, device(0, 1))

    w_cross().start()
    for d in (1, 2, 3):
        m_copy(d).start()
    h_copy(1).start()

    @pl.when(is_inner)
    def _():
        w_out(z, 0, True).start()
        w_across(z, 0, True).start()

    @pl.when(is_end)
    def _():
        w_in(z, 0, True).start()

    base_copy.start()
    local_h.wait()
    local_w.wait()
    w_cross().wait_recv()
    for d in (2, 3):
        h_copy(d).start()

    def spread(zp):
        e_chain(inward, 0, zp).wait_recv()
        for d in (1, 2, 3):
            e_plane(d, zp).start()

    def send_partials():
        pbuf[...] = acc[...].astype(jnp.bfloat16)
        for d in (3, 2, 1, 0):
            for other in range(2):
                if d or other:
                    p_copy(d, other).start()

    def shrink(zp, xr, size):
        number = (2 * zp + (1 - x if xr else x)).astype(jnp.float32)
        part = jnp.dot(
            hbuf[:, :, :size].reshape(4 * rows, size), wbuf[zp, xr, :size], preferred_element_type=jnp.float32
        ).reshape(4, rows, width)
        acc[...] = jnp.where(mbuf[...].astype(jnp.float32) == number, part, acc[...])

    def shrink_end(zp, xr):
        number = (2 * zp + (x + xr) % 2).astype(jnp.float32)
        part = jnp.dot(
            hbuf2[...].reshape(4 * rows, hi), wbuf[zp, xr, lo:], preferred_element_type=jnp.float32
        ).reshape(4, rows, width)
        acc2[...] = jnp.where(mbuf2[...].astype(jnp.float32) == number, part, acc2[...])

    @pl.when(is_inner)
    def _():
        zn, zo = z + outward, last - z
        zf = last - zn
        w_out(z, 1).start()
        w_across(zn, 0).wait_recv()
        w_across(zn, 0).start()
        w_across(zo, 0).wait_recv()
        w_out(z, 0, True).wait_send()
        e_chain(outward, 0, z, True).start()
        w_out(zo, 0).start()
        w_across(zn, 1).wait_recv()
        w_across(z, 0, True).wait_send()
        w_across(zn, 1).start()
        for d in (2, 3):
            e_plane(d, z, True).start()
        acc2[...] = jnp.zeros_like(acc2)
        w_across(zf, 0).wait_recv()
        w_out(z, 1).wait_send()
        w_out(zf, 0).start()
        spread(zn)
        w_across(zn, 0).wait_send()
        e_chain(-outward, 1, zn).start()
        e_chain(-outward, 1, z, True).start()
        w_across(z, 1).start()
        for d in (1, 2, 3):
            m_copy(d).wait_recv()
            h_copy(d).wait_recv()
        for zp, xr in ((z, 0), (z, 1), (zn, 0), (zn, 1), (zo, 0), (zf, 0)):
            shrink(zp, xr, chunk)
        w_across(zf, 1).wait_recv()
        w_out(zo, 0).wait_send()
        w_out(zf, 1).start()
        shrink(zf, 1, chunk)
        m2_copy().wait_recv()
        for d in range(4):
            hi_copy(d).wait_recv()

        lax.fori_loop(0, nz, lambda i, c: (shrink_end(i, 0), c)[1], 0)
        lax.fori_loop(1, nz, lambda i, c: (shrink_end((zo + i) % nz, 1), c)[1], 0)
        spread(zf)
        e_chain(outward, 0, zf).start()
        spread(zo)
        e_chain(outward, 0, zo).start()
        w_across(zo, 1).wait_recv()
        w_out(zf, 0).wait_send()
        w_out(zo, 1).start()
        shrink_end(zo, 1)
        pbuf2[...] = acc2[...].astype(jnp.bfloat16)
        a_copy().start()
        shrink(zo, 1, chunk)
        send_partials()

    @pl.when(is_end)
    def _():
        zi, zf = z + inward, last - z
        zo = last - zi
        w_in(z, 1).start()
        w_in(z, 0, True).wait_send()
        e_chain(inward, 0, z, True).start()
        hi_copy(0).start()
        h_copy(1).wait_recv()
        hi_copy(1).start()
        for d in (2, 3):
            e_plane(d, z, True).start()
        for d in (1, 2, 3):
            m_copy(d).wait_recv()
        m2_copy().start()
        for d in (2, 3):
            h_copy(d).wait_recv()
            hi_copy(d).start()
        w_in(z, 1).wait_send()
        shrink(z, 0, lo)
        shrink(z, 1, lo)
        for xr in range(2):
            w_got(zi, xr).wait_recv()
            shrink(zi, xr, lo)
        spread(zi)
        for zp, xr in ((zo, 0), (zf, 0), (zf, 1)):
            w_got(zp, xr).wait_recv()
            shrink(zp, xr, lo)
        spread(zf)
        spread(zo)
        w_got(zo, 1).wait_recv()
        shrink(zo, 1, lo)
        a_copy().wait_recv()
        acc[...] += abuf[...].astype(jnp.float32)
        send_partials()

    for copy in local_e:
        copy.wait()
    for k in range(1, nz):
        for d in (1, 2, 3):
            e_plane(d, (z + k) % nz).wait_recv()
    for d in (2, 3):
        e_plane(d, z, True).wait_recv()
    total = acc[0]
    for d in range(4):
        for other in range(2):
            if d or other:
                p_copy(d, other).wait_recv()
                total = total + rbuf[d, other].astype(jnp.float32)
    count = ebuf.shape[1] // rank
    total = total.astype(jnp.bfloat16)
    named = jnp.concatenate([mbuf[0].astype(jnp.float32)] * (count * rank // width), axis=1)
    chosen = named == (lax.broadcasted_iota(jnp.int32, (rows, count * rank), 1) // rank).astype(jnp.float32)
    for j in range(2):
        one = jnp.concatenate([total[:, j * rank:(j + 1) * rank]] * count, axis=1)
        spread = jnp.where(chosen, one.astype(jnp.float32), 0.0).astype(jnp.bfloat16)
        delta_ref[:, j, :] = jnp.dot(spread, ebuf[j], preferred_element_type=jnp.float32)

    @pl.when(is_end)
    def _():
        m2_copy().wait_send()
        for d in range(4):
            hi_copy(d).wait_send()
        e_chain(inward, 0, z, True).wait_send()

    @pl.when(is_inner)
    def _():
        zn, zo = z + outward, last - z
        zf = last - zn
        a_copy().wait_send()
        w_out(zo, 1).wait_send()
        w_out(zf, 1).wait_send()
        w_across(zn, 1).wait_send()
        w_across(z, 1).wait_send()
        for zp in (zo, zf):
            e_chain(outward, 0, zp).wait_send()
        e_chain(outward, 0, z, True).wait_send()
        e_chain(-outward, 1, zn).wait_send()
        e_chain(-outward, 1, z, True).wait_send()

    base_copy.wait()
    w_cross().wait_send()
    for d in (1, 2, 3):
        m_copy(d).wait_send()
        h_copy(d).wait_send()
    for d in (2, 3):
        e_plane(d, z, True).wait_send()
    for d in range(4):
        for other in range(2):
            if d or other:
                p_copy(d, other).wait_send()
    for k in range(1, nz):
        for d in (1, 2, 3):
            e_plane(d, (z + k) % nz).wait_send()


def local_planes(
    hidden, row_adapter_index, adapter_shrink_weight, adapter_expand_weight, base_partial_sums
):
    nz = lax.axis_size("adapter") // 2
    rows, width_here = hidden.shape
    chunk = width_here // 4
    hi = chunk * HI_EIGHTHS // 8
    width = adapter_shrink_weight.shape[2]
    rank, feats = adapter_expand_weight.shape[2:]
    dma = pltpu.SemaphoreType.DMA
    hbm = pl.BlockSpec(memory_space=pl.ANY)
    vmem = pl.BlockSpec(memory_space=pltpu.VMEM)
    bf16 = jnp.bfloat16
    delta, peer_base = pl.pallas_call(
        functools.partial(plane_kernel, nz),
        out_shape=(
            jax.ShapeDtypeStruct((rows, 2, feats), jnp.float32),
            jax.ShapeDtypeStruct((rows, 2, feats), bf16),
        ),
        in_specs=[hbm, vmem, hbm, hbm, hbm],
        out_specs=(vmem, hbm),
        scratch_shapes=[
            pltpu.VMEM((4, rows, chunk), bf16),
            pltpu.VMEM((4, rows, width), bf16),
            pltpu.VMEM((nz, 2, chunk, width), bf16),
            pltpu.VMEM((2, 2 * nz * rank, feats), bf16),
            pltpu.VMEM((4, rows, width), jnp.float32),
            pltpu.VMEM((4, rows, width), bf16),
            pltpu.VMEM((4, 2, rows, width), bf16),
            pltpu.VMEM((4, rows, hi), bf16),
            pltpu.VMEM((4, rows, width), bf16),
            pltpu.VMEM((4, rows, width), jnp.float32),
            pltpu.VMEM((4, rows, width), bf16),
            pltpu.VMEM((4, rows, width), bf16),
            dma((4,)), dma((4,)), dma((4,)), dma((4,)),
            dma, dma, dma((2, nz, 2)), dma((nz, 2)),
            dma((2, nz)), dma((nz,)), dma((nz, 4)), dma((nz, 4)),
            dma((4, 2)), dma((4, 2)), dma, dma, dma((4,)),
            dma((5,)), dma((5,)), dma, dma,
        ],
        compiler_params=pltpu.CompilerParams(
            collective_id=0, has_side_effects=True, vmem_limit_bytes=60 * 1024 * 1024
        ),
    )(hidden, row_adapter_index.reshape(1, rows), adapter_shrink_weight, adapter_expand_weight, base_partial_sums)
    own = lax.dynamic_slice_in_dim(base_partial_sums[0], lax.axis_index("tensor") * feats, feats, axis=2)
    return (own.astype(jnp.float32) + peer_base.astype(jnp.float32) + delta).astype(bf16)


def local(
    hidden, row_adapter_index, adapter_shrink_weight, adapter_expand_weight, base_partial_sums
):
    row_count = hidden.shape[0]
    owner_count = lax.axis_size("adapter")
    capacity = max(2, (2 * row_count + owner_count - 1) // owner_count)
    slot_count = owner_count * capacity
    row_owner = row_adapter_index[:, 0]
    owner_hot = (row_owner[:, None] == jnp.arange(owner_count, dtype=jnp.int32)[None, :]).astype(
        jnp.float32
    )
    earlier = (jnp.arange(row_count)[:, None] > jnp.arange(row_count)[None, :]).astype(jnp.float32)
    before = jnp.dot(earlier, owner_hot, precision=lax.Precision.HIGHEST)
    slot_index = jnp.sum(before * owner_hot, axis=1)
    slot_hot = (slot_index[:, None] == jnp.arange(capacity, dtype=jnp.float32)[None, :]).astype(
        jnp.float32
    )
    placing = (owner_hot[:, :, None] * slot_hot[:, None, :]).reshape(row_count, slot_count)
    outgoing = jnp.dot(placing.T.astype(jnp.bfloat16), hidden, preferred_element_type=jnp.float32)
    outgoing = outgoing.astype(jnp.bfloat16).reshape(owner_count, capacity, hidden.shape[1])
    shrink_factor_table = adapter_shrink_weight[0]
    rank_index = adapter_expand_weight.shape[2]
    expand_factor_table = adapter_expand_weight[0].astype(jnp.float32)
    shrunk = lax.psum(
        jnp.einsum(
            "ocw,wk->ock",
            lax.all_to_all(outgoing, "adapter", split_axis=0, concat_axis=0, tiled=True),
            shrink_factor_table,
            preferred_element_type=jnp.float32,
        ),
        "tensor",
    )
    shrunk = shrunk.reshape(shrunk.shape[0], shrunk.shape[1], 2, rank_index)
    delta = jnp.einsum(
        "ocjk,jkf->ocjf", shrunk, expand_factor_table, precision=lax.Precision.HIGHEST
    )
    returned = lax.all_to_all(delta, "adapter", split_axis=0, concat_axis=0, tiled=True)
    row_delta = jnp.einsum(
        "rs,sjf->rjf",
        placing,
        returned.reshape(slot_count, 2, returned.shape[3]),
        precision=lax.Precision.HIGHEST,
    )
    base_sum = lax.psum_scatter(
        base_partial_sums[0].astype(jnp.float32).astype(jnp.bfloat16),
        "tensor",
        scatter_dimension=2,
        tiled=True,
    ).astype(jnp.float32)
    return (base_sum + row_delta).astype(jnp.bfloat16)


def solution(mesh):
    in_specs = (
        P(("groups", "adapter"), "tensor"),
        P(("groups", "adapter"), None),
        P("adapter", "tensor", None),
        P("adapter", None, None, "tensor"),
        P("tensor", ("groups", "adapter"), None, None),
    )
    out_specs = P(("groups", "adapter"), None, "tensor")
    adapters = mesh.shape["adapter"]
    planes = (
        mesh.shape["groups"] == 2 and mesh.shape["tensor"] == 2 and adapters == 8
    )
    step = local_planes if planes else local
    return jax.shard_map(step, mesh=mesh, in_specs=in_specs, out_specs=out_specs, check_vma=False)
```
